128 devices in a mesh: row: 16 (over x, y), ck: 8 (over z, core).
Axes of the slice: x: 4, y: 4, z: 4, core: 2. Of those that a mesh axis runs over, the one named last changes fastest.
Arguments:
- amp_tiles: bfloat16 [16, 8, 16, 16, 128, 128], P('row', 'ck'), may hold values from -6 to 6
- tile_pos: int32 [16, 8, 16, 16], P(None, 'ck'), may hold values from 0 to 2303, as said below
- tile_count: int32 [16, 8, 16], P(None, 'ck'), may hold values from 0 to 16, as said below
- cycle_integrals: bfloat16 [294912, 512], P('ck'), may hold values from -0.046875 to 0.046875
- row_gap: float32 [16384], P(('row', 'ck')), may hold values from 0.5 to 4
- col_gap: float32 [512], replicated, may hold values from 0.5 to 4
Outputs:
- new_amp: bfloat16 [16384, 512], P(('row', 'ck'))
The draws below stay inside these ranges and needn't reach their ends.
Inputs may be any that keep to these rules, and one draw needn't show every extreme that they name: `tile_pos`: slots 0 to tile_count - 1 of each list are live, the others hold no tile. Within one ck group and one row owner all slots' positions are distinct. `tile_count`: in every ck group one row owner receives 16 live tiles from every storage owner.
All inputs are finite; a program needn't handle non-finite values.
Results may differ from the reference program's by a relative error of at most 0.001.
Values may be sent and summed in bfloat16 or wider, within the bound.
A program may use at most 320 MiB of HBM per device.

```python
import math
import jax
import jax.numpy as jnp
from jax import lax

TILE = 128
KT_DEV = 288
ROWT_DEV = 8
CAP = 16
COLS = 512
OWNERS = 16
GROUPS = 8
ROWS = 16384
CKROWS = 294912
N_ROW = 16
N_CK = 8


def tile_pattern(key):
    base_key = jax.random.fold_in(key, 7)
    place_key, count_key, full_key = jax.random.split(base_key, 3)
    total = ROWT_DEV * KT_DEV
    slot_total = OWNERS * CAP

    def one_list(sub_key):
        first_key, second_key = jax.random.split(sub_key)
        middle = (jax.random.permutation(first_key, total - 2) + 1).astype(jnp.int32)
        ordered = jnp.concatenate([jnp.array([0, total - 1], jnp.int32), middle])[:slot_total]
        return jax.random.permutation(second_key, ordered).astype(jnp.int32)
    list_keys = jax.random.split(place_key, GROUPS * OWNERS)
    lists = jax.vmap(one_list)(list_keys).reshape(GROUPS, OWNERS, OWNERS, CAP)
    positions = jnp.transpose(lists, (2, 0, 1, 3)).astype(jnp.int32)
    counts = jax.random.randint(count_key, (OWNERS, GROUPS, OWNERS), 0, CAP + 1)
    full_owner = jax.random.randint(full_key, (GROUPS,), 0, OWNERS)
    is_full = jnp.arange(OWNERS)[None, :] == full_owner[:, None]
    counts = jnp.where(is_full[None, :, :], CAP, counts).astype(jnp.int32)
    return (positions, counts)


def draw_tile_pos(key, part):
    return tile_pattern(key)[0]


def draw_tile_count(key, part):
    return tile_pattern(key)[1]


def block_levels(stream_key, dims, shards, least, top_value):
    factor_of, own = 1.0, jax.random.fold_in(stream_key, 6)
    for axis_at, parts in shards:
        draws = jnp.exp(jax.random.uniform(jax.random.fold_in(own, axis_at), (parts,), jnp.float32, least / len(shards), top_value / len(shards)))
        factor_of = factor_of * jnp.repeat(draws, dims[axis_at] // parts).reshape([-1 if axis == axis_at else 1 for axis in range(len(dims))])
    return factor_of


def normal_values(own_key, extent, deviation, reach, pieces=(), held_as=jnp.bfloat16):
    entries = jax.random.normal(own_key, extent, jnp.float32) * deviation
    if len(pieces) > 0:
        entries = block_levels(own_key, extent, pieces, -0.22, 0.18) * entries
    return jnp.clip(entries, min=-reach, max=reach).astype(held_as)


def setup_inputs(seed: int = 0) -> dict:
    splits = jax.random.split(jax.random.key(seed), 7)
    return {
        "amp_tiles": normal_values(splits[0], (OWNERS, GROUPS, OWNERS, CAP, TILE, TILE), 1.0, 6.0, ((0, 16), (1, 8))),
        "tile_pos": draw_tile_pos(jax.random.fold_in(splits[6], 71), 0),
        "tile_count": draw_tile_count(jax.random.fold_in(splits[6], 71), 0),
        "cycle_integrals": normal_values(splits[3], (CKROWS, COLS), (TILE * N_CK * CAP * N_ROW // (2 * ROWT_DEV)) ** -0.5, 0.046875, ((0, 8),)),
        "row_gap": jnp.clip(jnp.exp(math.log(4.0) - 2.0794415 * jax.random.uniform(splits[4], (ROWS,), jnp.float32) ** block_levels(splits[4], (ROWS,), ((0, 128),), -0.2, 0.2)), 0.5, 4.0),
        "col_gap": jnp.clip(jnp.exp(jax.random.uniform(splits[5], (COLS,), jnp.float32, math.log(0.5), math.log(4.0))), 0.5, 4.0),
    }


def reference(amp_tiles, tile_pos, tile_count, cycle_integrals, row_gap, col_gap):
    blocks = cycle_integrals.reshape(N_CK, KT_DEV, TILE, COLS)
    slot_range = jnp.arange(CAP, dtype=jnp.int32)
    tile_range = jnp.arange(ROWT_DEV, dtype=jnp.int32)

    def add_pair(totals, pair_index):
        group_index = pair_index // N_ROW
        owner_index = pair_index % N_ROW
        in_group = lax.dynamic_index_in_dim(amp_tiles, group_index, 1, keepdims=False)
        amp_slots = lax.dynamic_index_in_dim(in_group, owner_index, 1, keepdims=False).reshape(N_ROW * CAP, TILE, TILE)
        pos_group = lax.dynamic_index_in_dim(tile_pos, group_index, 1, keepdims=False)
        positions = lax.dynamic_index_in_dim(pos_group, owner_index, 1, keepdims=False).reshape(-1)
        count_group = lax.dynamic_index_in_dim(tile_count, group_index, 1, keepdims=False)
        counts = lax.dynamic_index_in_dim(count_group, owner_index, 1, keepdims=False).reshape(-1)
        live_mask = (slot_range[None, :] < counts[:, None]).reshape(-1)
        group_blocks = lax.dynamic_index_in_dim(blocks, group_index, 0, keepdims=False)
        picked = group_blocks[positions % KT_DEV]
        products = jnp.einsum("mrk,mkc->mrc", amp_slots.astype(jnp.float32), picked.astype(jnp.float32), precision=lax.Precision.HIGHEST)
        selector = ((positions // KT_DEV)[None, :] == tile_range[:, None]) & live_mask[None, :]
        summed = jnp.einsum("im,mrc->irc", selector.astype(jnp.float32), products, precision=lax.Precision.HIGHEST)
        summed = summed.reshape(ROWT_DEV * TILE, COLS)
        row_start = (owner_index * (ROWT_DEV * TILE)).astype(jnp.int32)
        current = lax.dynamic_slice_in_dim(totals, row_start, ROWT_DEV * TILE, 0)
        return lax.dynamic_update_slice_in_dim(totals, current + summed, row_start, 0), None

    initial = jnp.zeros((ROWS, COLS), jnp.float32)
    totals = lax.scan(add_pair, initial, jnp.arange(N_CK * N_ROW, dtype=jnp.int32))[0]
    update = (totals / (row_gap[:, None] + col_gap[None, :])).astype(jnp.bfloat16)
    piece_rows = ROWT_DEV * TILE // (N_CK * N_ROW)
    reordered = update.reshape(N_ROW, N_CK, N_ROW, piece_rows, COLS).transpose(2, 1, 0, 3, 4)
    return reordered.reshape(ROWS, COLS)
```

```python
import math

import jax
import jax.numpy as jnp
from jax import lax
from jax.experimental import pallas as pl
from jax.experimental.pallas import tpu as pltpu
from jax.sharding import PartitionSpec as P

TILE = 128
KT_DEV = 288
ROWT_DEV = 8
CAP = 16
COLS = 512
HALF = COLS // 2
MESH = pl.DeviceIdType.MESH

SIDE = 4
ITEMS = 16
LAG1, LAG2, LAG3 = 3, 2, 1
KEEP = LAG1 + LAG2
SLOTS = 4
W_PARTS = 8

LEVELS = 32000.0
STEPS = 256.0
LN2 = math.log(2.0)
FLOOR = 2.0**-100


def pick(a):
    return lax.div(2 - a, 2), lax.rem(a, 2), lax.div(a, 2)


def scale_code(top):
    level = jnp.ceil(jnp.log(jnp.maximum(top, FLOOR)) * (STEPS / LN2))
    return level.astype(jnp.int32).astype(jnp.int16), jnp.exp(level * (-LN2 / STEPS)) * LEVELS


def scale_value(code):
    level = code.astype(jnp.int32).astype(jnp.float32)
    return jnp.exp(level * (LN2 / STEPS)) * (1.0 / LEVELS)


def encode(block, inverse):
    return jnp.round(block * inverse).astype(jnp.int32).astype(jnp.int16)


def decode(block, scale):
    return block.astype(jnp.int32).astype(jnp.float32) * scale


def kernel(
    ck_ref, prev_ref, last_ref, rowgap_ref, colgap_ref, amp_ref, w_ref, out_ref,
    w_v, amp_v, acc, own, csend, crecv, keep, s1send, s1recv, s2send, s2recv, cbuf, s3recv, fin,
    w_sem, amp_sem, c_ssem, c_rsem, s1_ssem, s1_rsem, s2_ssem, s2_rsem, s3_ssem, s3_rsem, credit,
):
    row, ck = lax.axis_index("row"), lax.axis_index("ck")
    x, y = lax.div(row, SIDE), lax.rem(row, SIDE)
    z, core = lax.div(ck, 2), lax.rem(ck, 2)
    partner = (row, z * 2 + (1 - core))

    def w_copy(part):
        span = pl.ds(part * (KT_DEV // W_PARTS), KT_DEV // W_PARTS)
        return pltpu.make_async_copy(w_ref.at[span], w_v.at[span], w_sem.at[part])

    def amp_copy(item):
        slot = lax.rem(item, 2)
        return pltpu.make_async_copy(amp_ref.at[item], amp_v.at[slot], amp_sem.at[slot])

    for part in range(W_PARTS):
        w_copy(part).start()
    amp_copy(0).start()

    def on_axis(a):
        e0, e1, e2 = pick(a)
        return e0 * z + e1 * x + e2 * y

    def axis_peer(a, d):
        e0, e1, e2 = pick(a)
        mine = e0 * z + e1 * x + e2 * y
        shift = lax.rem(mine + d, SIDE) - mine
        return ((x + e1 * shift) * SIDE + y + e2 * shift, (z + e0 * shift) * 2 + core)

    def axis_of(item, stage):
        return lax.rem(lax.rem(item, 3) + stage, 3)

    barrier = pltpu.get_barrier_semaphore()
    pl.semaphore_signal(barrier, inc=1, device_id=partner, device_id_type=MESH)
    for a in range(3):
        for d in range(1, SIDE):
            pl.semaphore_signal(barrier, inc=1, device_id=axis_peer(a, d), device_id_type=MESH)
    pl.semaphore_wait(barrier, 10)

    acc[CAP] = jnp.zeros((TILE, HALF), jnp.float32)
    for part in range(W_PARTS):
        w_copy(part).wait()

    def c_copy(item):
        slot = lax.rem(item, 2)
        return pltpu.make_async_remote_copy(
            src_ref=csend.at[slot], dst_ref=crecv.at[slot], send_sem=c_ssem.at[slot], recv_sem=c_rsem.at[slot],
            device_id=partner, device_id_type=MESH,
        )

    def s1_copy(item, d):
        slot = lax.rem(item, SLOTS)
        return pltpu.make_async_remote_copy(
            src_ref=s1send.at[slot, d - 1], dst_ref=s1recv.at[item, d - 1],
            send_sem=s1_ssem.at[slot, d - 1], recv_sem=s1_rsem.at[item, d - 1],
            device_id=axis_peer(axis_of(item, 0), d), device_id_type=MESH,
        )

    def s2_copy(item, d):
        slot = lax.rem(item, SLOTS)
        return pltpu.make_async_remote_copy(
            src_ref=s2send.at[slot, d - 1], dst_ref=s2recv.at[item, d - 1],
            send_sem=s2_ssem.at[slot, d - 1], recv_sem=s2_rsem.at[item, d - 1],
            device_id=axis_peer(axis_of(item, 1), d), device_id_type=MESH,
        )

    def s3_copy(item, d):
        slot = lax.rem(item, SLOTS)
        a = axis_of(item, 2)
        return pltpu.make_async_remote_copy(
            src_ref=cbuf.at[slot, lax.rem(on_axis(a) + d, SIDE)], dst_ref=s3recv.at[item, d - 1],
            send_sem=s3_ssem.at[slot, d - 1], recv_sem=s3_rsem.at[item, d - 1],
            device_id=axis_peer(a, d), device_id_type=MESH,
        )

    def compute(item):
        slot = lax.rem(item, 2)

        @pl.when(item + 1 < ITEMS)
        def _():
            amp_copy(item + 1).start()

        amp_copy(item).wait()

        @pl.when(item >= 2)
        def _():
            c_copy(item - 2).wait_send()

        kind = lax.rem(item, 3)
        strides = []
        for a in range(3):
            e0, e1, e2 = pick(lax.rem(a - kind + 3, 3))
            strides.append(e0 * 16 + e1 * 4 + e2)
        sz, sx, sy = strides
        for h in range(2):
            for j in range(CAP):
                at = item * CAP + j
                product = jnp.dot(
                    amp_v[slot, j], w_v[ck_ref[at], :, h * HALF : (h + 1) * HALF], preferred_element_type=jnp.float32
                )
                acc[j] = product + acc[prev_ref[at]]

            def spread(tz, carry):
                for side, target in ((core, own), (1 - core, csend)):
                    source = last_ref[item * ROWT_DEV + tz * 2 + side]
                    for tx in range(SIDE):
                        for ty in range(SIDE):
                            at = tx * SIDE + ty
                            place = tz * sz + tx * sx + ty * sy
                            target[slot, place, h * 8 : (h + 1) * 8] = acc[source, at * 8 : (at + 1) * 8]
                return carry

            lax.fori_loop(0, SIDE, spread, 0)

        @pl.when(item >= 2)
        def _():
            pl.semaphore_wait(credit, 1)

        c_copy(item).start()

    def stage1(item):
        slot, kslot, sslot = lax.rem(item, 2), lax.rem(item, KEEP), lax.rem(item, SLOTS)
        mine = on_axis(axis_of(item, 0))
        c_copy(item).wait_recv()

        @pl.when(item >= SLOTS)
        def _():
            for d in range(1, SIDE):
                s1_copy(item - SLOTS, d).wait_send()

        for d in (2, 1, 3):
            base = lax.rem(mine + d, SIDE) * 16
            top = jnp.zeros((16, HALF), jnp.float32)
            for b in range(16):
                total = own[slot, base + b] + crecv[slot, base + b]
                own[slot, base + b] = total
                top = jnp.maximum(top, jnp.abs(total))
            code, inverse = scale_code(top)
            for b in range(16):
                s1send[sslot, d - 1, b] = encode(own[slot, base + b], inverse)
            s1send[sslot, d - 1, 16] = code
            s1_copy(item, d).start()
        base = mine * 16
        for b in range(16):
            keep[kslot, b] = own[slot, base + b] + crecv[slot, base + b]

        @pl.when(item < ITEMS - 2)
        def _():
            pl.semaphore_signal(credit, inc=1, device_id=partner, device_id_type=MESH)

    def stage2(item):
        kslot, sslot = lax.rem(item, KEEP), lax.rem(item, SLOTS)
        mine = on_axis(axis_of(item, 1))
        for d in range(1, SIDE):
            s1_copy(item, d).wait_recv()

        @pl.when(item >= SLOTS)
        def _():
            for d in range(1, SIDE):
                s2_copy(item - SLOTS, d).wait_send()

        scales = [scale_value(s1recv[item, d, 16]) for d in range(3)]

        def total_of(at):
            total = keep[kslot, at]
            for d in range(3):
                total = total + decode(s1recv[item, d, at], scales[d])
            return total

        for d in range(1, SIDE):
            base = lax.rem(mine + d, SIDE) * SIDE
            top = jnp.zeros((16, HALF), jnp.float32)
            for b in range(SIDE):
                total = total_of(base + b)
                keep[kslot, base + b] = total
                top = jnp.maximum(top, jnp.abs(total))
            code, inverse = scale_code(top)
            for b in range(SIDE):
                s2send[sslot, d - 1, b] = encode(keep[kslot, base + b], inverse)
            s2send[sslot, d - 1, SIDE] = code
            s2_copy(item, d).start()
        for b in range(SIDE):
            keep[kslot, mine * SIDE + b] = total_of(mine * SIDE + b)

    def stage3(item):
        kslot, sslot = lax.rem(item, KEEP), lax.rem(item, SLOTS)
        mine = on_axis(axis_of(item, 1))
        for d in range(1, SIDE):
            s2_copy(item, d).wait_recv()

        @pl.when(item >= SLOTS)
        def _():
            for d in range(1, SIDE):
                s3_copy(item - SLOTS, d).wait_send()

        scales = [scale_value(s2recv[item, d, SIDE]) for d in range(3)]
        for b in range(SIDE):
            total = keep[kslot, mine * SIDE + b]
            for d in range(3):
                total = total + decode(s2recv[item, d, b], scales[d])
            cbuf[sslot, b] = total
        for d in range(1, SIDE):
            s3_copy(item, d).start()

    def finish(item):
        sslot = lax.rem(item, SLOTS)
        mine = on_axis(axis_of(item, 2))
        for d in range(1, SIDE):
            s3_copy(item, d).wait_recv()
        total = cbuf[sslot, mine]
        for d in range(3):
            total = total + s3recv[item, d]
        fin[item, :, :HALF] = total[:8]
        fin[item, :, HALF:] = total[8:]

    def step(t, carry):
        pl.when(t < ITEMS)(lambda: compute(t))
        for first, body in (
            (1 + LAG1 + LAG2 + LAG3, finish),
            (1 + LAG1 + LAG2, stage3),
            (1 + LAG1, stage2),
            (1, stage1),
        ):
            pl.when((t >= first) & (t < first + ITEMS))(lambda first=first, body=body: body(t - first))
        return carry

    lax.fori_loop(0, ITEMS + 1 + LAG1 + LAG2 + LAG3, step, 0)

    def drain(item, carry):
        for d in range(1, SIDE):
            s1_copy(item, d).wait_send()
            s2_copy(item, d).wait_send()
            s3_copy(item, d).wait_send()
        return carry

    lax.fori_loop(ITEMS - SLOTS, ITEMS, drain, 0)
    for item in (ITEMS - 2, ITEMS - 1):
        c_copy(item).wait_send()
    gaps = rowgap_ref[...].reshape(ITEMS, 8, 1) + colgap_ref[...].reshape(1, 1, COLS)
    out_ref[...] = (fin[...] / gaps).reshape(ITEMS * 8, COLS).astype(jnp.bfloat16)


def on_device(amp_tiles, tile_pos, tile_count, cycle_integrals, row_gap, col_gap):
    my_row = lax.axis_index("row")
    positions = lax.dynamic_index_in_dim(tile_pos, my_row, 0, keepdims=False).reshape(ITEMS, CAP)
    counts = lax.dynamic_index_in_dim(tile_count, my_row, 0, keepdims=False).reshape(ITEMS)
    slots = jnp.arange(CAP, dtype=jnp.int32)
    live = slots[None, :] < counts[:, None]
    row_tile = jnp.where(live, positions // KT_DEV, -1)
    same = (row_tile[:, None, :] == row_tile[:, :, None]) & (slots[None, None, :] < slots[None, :, None])
    before = jnp.max(jnp.where(same, slots[None, None, :], -1), axis=2)
    before = jnp.where(before < 0, CAP, before).reshape(-1)
    mine = row_tile[:, None, :] == jnp.arange(ROWT_DEV, dtype=jnp.int32)[None, :, None]
    last = jnp.max(jnp.where(mine, slots[None, None, :], -1), axis=2)
    last = jnp.where(last < 0, CAP, last).reshape(-1)
    ck_tile = (positions % KT_DEV).reshape(-1)
    gaps = lax.all_to_all(row_gap.reshape(ITEMS, 8), "row", split_axis=0, concat_axis=0, tiled=True)

    f32, i16, bf16 = jnp.float32, jnp.int16, jnp.bfloat16
    smem = pl.BlockSpec(memory_space=pltpu.SMEM)
    vmem = pl.BlockSpec(memory_space=pltpu.VMEM)
    hbm = pl.BlockSpec(memory_space=pl.ANY)
    dma = pltpu.SemaphoreType.DMA
    return pl.pallas_call(
        kernel,
        out_shape=jax.ShapeDtypeStruct((ITEMS * 8, COLS), bf16),
        in_specs=[smem, smem, smem, vmem, vmem, hbm, hbm],
        out_specs=vmem,
        scratch_shapes=[
            pltpu.VMEM((KT_DEV, TILE, COLS), bf16),
            pltpu.VMEM((2, CAP, TILE, TILE), bf16),
            pltpu.VMEM((CAP + 1, TILE, HALF), f32),
            pltpu.VMEM((2, 64, 16, HALF), f32),
            pltpu.VMEM((2, 64, 16, HALF), f32),
            pltpu.VMEM((2, 64, 16, HALF), f32),
            pltpu.VMEM((KEEP, 16, 16, HALF), f32),
            pltpu.VMEM((SLOTS, 3, 17, 16, HALF), i16),
            pltpu.VMEM((ITEMS, 3, 17, 16, HALF), i16),
            pltpu.VMEM((SLOTS, 3, 5, 16, HALF), i16),
            pltpu.VMEM((ITEMS, 3, 5, 16, HALF), i16),
            pltpu.VMEM((SLOTS, SIDE, 16, HALF), f32),
            pltpu.VMEM((ITEMS, 3, 16, HALF), f32),
            pltpu.VMEM((ITEMS, 8, COLS), f32),
            dma((W_PARTS,)),
            dma((2,)),
            dma((2,)),
            dma((2,)),
            dma((SLOTS, 3)),
            dma((ITEMS, 3)),
            dma((SLOTS, 3)),
            dma((ITEMS, 3)),
            dma((SLOTS, 3)),
            dma((ITEMS, 3)),
            pltpu.SemaphoreType.REGULAR,
        ],
        compiler_params=pltpu.CompilerParams(
            collective_id=0, has_side_effects=True, vmem_limit_bytes=63 * 1024 * 1024
        ),
        name="cycle_reduce",
    )(
        ck_tile,
        before,
        last,
        gaps.reshape(ITEMS * 8, 1),
        col_gap.reshape(1, COLS),
        amp_tiles.reshape(ITEMS, CAP, TILE, TILE),
        cycle_integrals.reshape(KT_DEV, TILE, COLS),
    )


def solution(mesh):
    return jax.shard_map(
        on_device,
        mesh=mesh,
        in_specs=(
            P("row", "ck", None, None, None, None),
            P(None, "ck", None, None),
            P(None, "ck", None),
            P("ck", None),
            P(("row", "ck")),
            P(),
        ),
        out_specs=P(("row", "ck"), None),
        check_vma=False,
    )
```

```python
import math

import jax
import jax.numpy as jnp
from jax import lax
from jax.experimental import pallas as pl
from jax.experimental.pallas import tpu as pltpu
from jax.sharding import PartitionSpec as P

TILE = 128
KT_DEV = 288
ROWT_DEV = 8
CAP = 16
COLS = 512
OWNERS = 16
HALF = COLS // 2
MESH = pl.DeviceIdType.MESH

SIDE = 4
PAIRS = OWNERS // 2
ITEMS = 2 * PAIRS
LAG_C, LAG_1A, LAG_1B, LAG_2A, LAG_2B, LAG_3 = 1, 4, 4, 4, 5, 5
OWN = LAG_1A + LAG_C
KEEP = LAG_1B + LAG_2A
CBUF = LAG_2B + LAG_3
SLOTS = 4
LAND = LAG_1A + LAG_1B
W_PARTS = 4
AROUND = (1, 3)

LEVELS = 32000.0
STEPS = 256.0
LN2 = math.log(2.0)
FLOOR = 2.0**-100


def pick(a):
    return lax.div(2 - a, 2), lax.rem(a, 2), lax.div(a, 2)


def scale_code(top):
    level = jnp.ceil(jnp.log(jnp.maximum(top, FLOOR)) * (STEPS / LN2))
    return level.astype(jnp.int32).astype(jnp.int16), jnp.exp(level * (-LN2 / STEPS)) * LEVELS


def scale_value(code):
    level = code.astype(jnp.int32).astype(jnp.float32)
    return jnp.exp(level * (LN2 / STEPS)) * (1.0 / LEVELS)


def encode(block, inverse):
    return jnp.round(block * inverse).astype(jnp.int32).astype(jnp.int16)


def decode(block, scale):
    return block.astype(jnp.int32).astype(jnp.float32) * scale


def send_code(read, count, target):
    top = jnp.abs(read(0))
    for b in range(1, count):
        top = jnp.maximum(top, jnp.abs(read(b)))
    code, inverse = scale_code(top)
    for b in range(count):
        target[b] = encode(read(b), inverse)
    target[count] = code


def kernel(
    pos_ref, count_ref, rowgap_ref, colgap_ref, amp_ref, w_ref, out_ref,
    pos_s, count_s, ck_s, prev_s, last_s,
    w0_v, w1_v, amp_v, acc, own, csend, crecv, keep, a1send, a1recv, b1send, b1recv,
    a2send, a2recv, b2send, b2recv, cbuf, s3recv, fin, gap0, gap1, gap2,
    t_sem, w_sem, amp_sem, c_ssem, c_rsem, a1_ssem, a1_rsem, b1_ssem, b1_rsem,
    a2_ssem, a2_rsem, b2_ssem, b2_rsem, s3_ssem, s3_rsem, g1_ssem, g1_rsem, g2_ssem, g2_rsem, credit,
):
    row, ck = lax.axis_index("row"), lax.axis_index("ck")
    x, y = lax.div(row, SIDE), lax.rem(row, SIDE)
    z, core = lax.div(ck, 2), lax.rem(ck, 2)
    partner = (row, z * 2 + (1 - core))

    def w_copy(h, part):
        span = pl.ds(part * (KT_DEV // W_PARTS), KT_DEV // W_PARTS)
        return pltpu.make_async_copy(
            w_ref.at[span, :, h * HALF : (h + 1) * HALF], (w0_v, w1_v)[h].at[span], w_sem.at[h, part]
        )

    def amp_copy(item):
        slot = lax.rem(item, 2)
        return pltpu.make_async_copy(amp_ref.at[pl.ds(lax.rem(item, PAIRS) * 2, 2)], amp_v.at[slot], amp_sem.at[slot])

    pos_copy = pltpu.make_async_copy(pos_ref.at[row, 0], pos_s, t_sem.at[0])
    count_copy = pltpu.make_async_copy(count_ref.at[row], count_s, t_sem.at[1])
    pos_copy.start()
    count_copy.start()
    for h in range(2):
        for part in range(W_PARTS):
            w_copy(h, part).start()
        if h == 0:
            amp_copy(0).start()

    def on_axis(a):
        e0, e1, e2 = pick(a)
        return e0 * z + e1 * x + e2 * y

    def axis_peer(a, d):
        e0, e1, e2 = pick(a)
        mine = e0 * z + e1 * x + e2 * y
        shift = lax.rem(mine + d, SIDE) - mine
        return ((x + e1 * shift) * SIDE + y + e2 * shift, (z + e0 * shift) * 2 + core)

    def axis_of(item, stage):
        return lax.rem(lax.rem(item, 3) + stage, 3)

    barrier = pltpu.get_barrier_semaphore()
    pl.semaphore_signal(barrier, inc=1, device_id=partner, device_id_type=MESH)
    for a in range(3):
        for d in range(1, SIDE):
            pl.semaphore_signal(barrier, inc=1, device_id=axis_peer(a, d), device_id_type=MESH)

    lanes = lax.broadcasted_iota(jnp.int32, (8, TILE), 1)
    rows = lax.broadcasted_iota(jnp.int32, (8, TILE), 0)
    gap_row = jnp.broadcast_to(rowgap_ref[...], (8, TILE))
    for r in range(OWNERS):
        value = jnp.sum(jnp.where(lanes == rows + r * 8, gap_row, 0.0), axis=1, keepdims=True)
        gap0[r] = jnp.broadcast_to(value, (8, TILE))
    for b in range(SIDE):
        gap1[x, b] = gap0[x * SIDE + b]
    acc[CAP] = jnp.zeros((TILE, HALF), jnp.float32)
    pl.semaphore_wait(barrier, 10)

    def gap1_copy(d):
        return pltpu.make_async_remote_copy(
            src_ref=gap0.at[pl.ds(lax.rem(x + d, SIDE) * SIDE, SIDE)], dst_ref=gap1.at[x],
            send_sem=g1_ssem.at[d - 1], recv_sem=g1_rsem.at[d - 1], device_id=axis_peer(1, d), device_id_type=MESH,
        )

    def gap1_arrived(d):
        return pltpu.make_async_remote_copy(
            src_ref=gap0.at[pl.ds(0, SIDE)], dst_ref=gap1.at[lax.rem(x + SIDE - d, SIDE)],
            send_sem=g1_ssem.at[d - 1], recv_sem=g1_rsem.at[d - 1], device_id=axis_peer(1, d), device_id_type=MESH,
        )

    def gap2_copy(d):
        return pltpu.make_async_remote_copy(
            src_ref=gap1.at[:, lax.rem(y + d, SIDE)], dst_ref=gap2.at[y],
            send_sem=g2_ssem.at[d - 1], recv_sem=g2_rsem.at[d - 1], device_id=axis_peer(2, d), device_id_type=MESH,
        )

    def gap2_arrived(d):
        return pltpu.make_async_remote_copy(
            src_ref=gap1.at[:, 0], dst_ref=gap2.at[lax.rem(y + SIDE - d, SIDE)],
            send_sem=g2_ssem.at[d - 1], recv_sem=g2_rsem.at[d - 1], device_id=axis_peer(2, d), device_id_type=MESH,
        )

    for d in range(1, SIDE):
        gap1_copy(d).start()

    pos_copy.wait()
    count_copy.wait()

    def tables(owner, carry):
        live = count_s[0, owner]
        tiles = []
        for j in range(CAP):
            position = pos_s[owner, j]
            row_tile = lax.div(position, KT_DEV)
            ck_s[owner * CAP + j] = position - row_tile * KT_DEV
            row_tile = jnp.where(j < live, row_tile, -1 - j)
            before = jnp.int32(CAP)
            for k in range(j):
                before = jnp.where(tiles[k] == row_tile, k, before)
            prev_s[owner * CAP + j] = before
            tiles.append(row_tile)
        for i in range(ROWT_DEV):
            last = jnp.int32(CAP)
            for k in range(CAP):
                last = jnp.where(tiles[k] == i, k, last)
            last_s[owner * ROWT_DEV + i] = last
        return carry

    lax.fori_loop(0, OWNERS, tables, 0)

    for d in range(1, SIDE):
        gap1_arrived(d).wait_recv()
    for b in range(SIDE):
        gap2[y, b] = gap1[b, y]
    for d in range(1, SIDE):
        gap2_copy(d).start()

    def c_copy(item, r):
        slot = lax.rem(item, 2)
        return pltpu.make_async_remote_copy(
            src_ref=csend.at[slot, r], dst_ref=crecv.at[slot, r], send_sem=c_ssem.at[slot, r],
            recv_sem=c_rsem.at[slot, r], device_id=partner, device_id_type=MESH,
        )

    def ring_copy(item, way, stage, source, target, ssem, rsem, slots=ITEMS):
        slot, land = lax.rem(item, SLOTS), lax.rem(item, slots)
        return pltpu.make_async_remote_copy(
            src_ref=source.at[slot, way], dst_ref=target.at[land, way], send_sem=ssem.at[slot, way],
            recv_sem=rsem.at[land, way], device_id=axis_peer(axis_of(item, stage), AROUND[way]), device_id_type=MESH,
        )

    def a1_copy(item, way):
        return ring_copy(item, way, 0, a1send, a1recv, a1_ssem, a1_rsem)

    def b1_copy(item, way):
        return ring_copy(item, way, 0, b1send, b1recv, b1_ssem, b1_rsem, LAND)

    def a2_copy(item, way):
        return ring_copy(item, way, 1, a2send, a2recv, a2_ssem, a2_rsem)

    def b2_copy(item, way):
        return ring_copy(item, way, 1, b2send, b2recv, b2_ssem, b2_rsem)

    def s3_copy(item, d):
        slot = lax.rem(item, CBUF)
        a = axis_of(item, 2)
        return pltpu.make_async_remote_copy(
            src_ref=cbuf.at[slot, lax.rem(on_axis(a) + d, SIDE)], dst_ref=s3recv.at[item, d - 1],
            send_sem=s3_ssem.at[slot, d - 1], recv_sem=s3_rsem.at[item, d - 1],
            device_id=axis_peer(a, d), device_id_type=MESH,
        )

    def sent_before(item, copy, slots):
        @pl.when(item >= slots)
        def _():
            for way in range(2):
                copy(item - slots, way).wait_send()

    def compute(item):
        slot, oslot = lax.rem(item, 2), lax.rem(item, OWN)
        h, pair = lax.div(item, PAIRS), lax.rem(item, PAIRS)

        @pl.when(item + 1 < ITEMS)
        def _():
            amp_copy(item + 1).start()

        for half in range(2):

            @pl.when(item == half * PAIRS)
            def _():
                for part in range(W_PARTS):
                    w_copy(half, part).wait()

        amp_copy(item).wait()
        sent_before(item, c_copy, 2)

        @pl.when(item >= 2)
        def _():
            pl.semaphore_wait(credit, 1)

        kind = lax.rem(item, 3)
        strides = []
        for a in range(3):
            e0, e1, e2 = pick(lax.rem(a - kind + 3, 3))
            strides.append(e0 * 16 + e1 * 4 + e2)
        sz, sx, sy = strides
        for r in range(2):
            owner = pair * 2 + r
            for half, w_v in enumerate((w0_v, w1_v)):

                @pl.when(h == half)
                def _():
                    for j in range(CAP):
                        at = owner * CAP + j
                        product = jnp.dot(amp_v[slot, r, j], w_v[ck_s[at]], preferred_element_type=jnp.float32)
                        acc[j] = product + acc[prev_s[at]]

            def spread(tz, carry):
                for side in range(2):
                    source = last_s[owner * ROWT_DEV + tz * 2 + (core if side == 0 else 1 - core)]
                    for tx in range(SIDE):
                        for ty in range(SIDE):
                            at = tx * SIDE + ty
                            place = tz * sz + tx * sx + ty * sy
                            if side == 0:
                                own[oslot, place, r * 8 : (r + 1) * 8] = acc[source, at * 8 : (at + 1) * 8]
                            else:
                                csend[slot, r, place] = acc[source, at * 8 : (at + 1) * 8]
                return carry

            lax.fori_loop(0, SIDE, spread, 0)
            c_copy(item, r).start()

    def stage1a(item):
        slot, oslot, sslot = lax.rem(item, 2), lax.rem(item, OWN), lax.rem(item, SLOTS)
        mine = on_axis(axis_of(item, 0))
        for r in range(2):
            c_copy(item, r).wait_recv()
        sent_before(item, a1_copy, SLOTS)

        def both(at):
            for r in range(2):
                own[oslot, at, r * 8 : (r + 1) * 8] += crecv[slot, r, at]

        base = lax.rem(mine + 2, SIDE) * 16
        for way in range(2):
            start = base + way * 8
            for b in range(8):
                both(start + b)
            send_code(lambda b, start=start: own[oslot, start + b], 8, a1send.at[sslot, way])
            a1_copy(item, way).start()

        def rest(d, carry):
            at = lax.rem(mine + 3 + d, SIDE) * 16
            for b in range(16):
                both(at + b)
            return carry

        lax.fori_loop(0, 3, rest, 0)

        @pl.when(item < ITEMS - 2)
        def _():
            pl.semaphore_signal(credit, inc=1, device_id=partner, device_id_type=MESH)

    def pass_on(item, count, stage, source, arrived, sending, copy_a, copy_b):
        sslot = lax.rem(item, SLOTS)
        mine = on_axis(axis_of(item, stage))
        for way in range(2):
            copy_a(item, way).wait_recv()
        sent_before(item, copy_b, SLOTS)
        part = count // 2
        for way in range(2):
            base = lax.rem(mine + AROUND[way], SIDE) * count
            scale = scale_value(arrived[item, way, part])
            for b in range(part):
                source[base + way * part + b] += decode(arrived[item, way, b], scale)
            send_code(lambda b, base=base: source[base + b], count, sending.at[sslot, way])
            copy_b(item, way).start()
        return mine * count

    def stage1b(item):
        source = own.at[lax.rem(item, OWN)]
        base = pass_on(item, 16, 0, source, a1recv, b1send, a1_copy, b1_copy)
        kslot = lax.rem(item, KEEP)
        for b in range(16):
            keep[kslot, b] = source[base + b]

    def stage2a(item):
        source, sslot, land = keep.at[lax.rem(item, KEEP)], lax.rem(item, SLOTS), lax.rem(item, LAND)
        mine = on_axis(axis_of(item, 1))
        for way in range(2):
            b1_copy(item, way).wait_recv()
        sent_before(item, a2_copy, SLOTS)
        up, down = [scale_value(b1recv[land, way, 16]) for way in range(2)]

        def both(at):
            source[at] += decode(b1recv[land, 0, at], up) + decode(b1recv[land, 1, at], down)

        base = lax.rem(mine + 2, SIDE) * SIDE
        for b in range(SIDE):
            both(base + b)
        for way in range(2):
            start = base + way * 2
            send_code(lambda b, start=start: source[start + b], 2, a2send.at[sslot, way])
            a2_copy(item, way).start()
        for d in (3, 0, 1):
            base = lax.rem(mine + d, SIDE) * SIDE
            for b in range(SIDE):
                both(base + b)

    def stage2b(item):
        source, cslot = keep.at[lax.rem(item, KEEP)], lax.rem(item, CBUF)
        base = pass_on(item, SIDE, 1, source, a2recv, b2send, a2_copy, b2_copy)

        @pl.when(item >= CBUF)
        def _():
            for d in range(1, SIDE):
                s3_copy(item - CBUF, d).wait_send()

        for b in range(SIDE):
            cbuf[cslot, b] = source[base + b]

    def stage3(item):
        cslot = lax.rem(item, CBUF)
        for way in range(2):
            b2_copy(item, way).wait_recv()
        up, down = [scale_value(b2recv[item, way, SIDE]) for way in range(2)]
        for b in range(SIDE):
            cbuf[cslot, b] += decode(b2recv[item, 0, b], up) + decode(b2recv[item, 1, b], down)
        for d in range(1, SIDE):
            s3_copy(item, d).start()

    def finish(item):
        for d in range(1, SIDE):
            s3_copy(item, d).wait_recv()
        total = cbuf[lax.rem(item, CBUF), on_axis(axis_of(item, 2))]
        for d in range(3):
            total = total + s3recv[item, d]
        fin[item] = total

    stages = []
    lag = LAG_C
    for body, after in (
        (stage1a, LAG_1A), (stage1b, LAG_1B), (stage2a, LAG_2A), (stage2b, LAG_2B), (stage3, LAG_3), (finish, 0),
    ):
        stages.append((lag, body))
        lag += after
    order = [*reversed(stages[1:]), (0, compute), stages[0]]

    def step(t, carry):
        for first, body in order:
            pl.when((t >= first) & (t < first + ITEMS))(lambda first=first, body=body: body(t - first))
        return carry

    lax.fori_loop(0, ITEMS + lag, step, 0)

    def drain(item, carry):
        for way in range(2):
            for copy in (a1_copy, b1_copy, a2_copy, b2_copy):
                copy(item, way).wait_send()
        return carry

    lax.fori_loop(ITEMS - SLOTS, ITEMS, drain, 0)

    def drain3(item, carry):
        for d in range(1, SIDE):
            s3_copy(item, d).wait_send()
        return carry

    lax.fori_loop(ITEMS - CBUF, ITEMS, drain3, 0)
    for item in (ITEMS - 2, ITEMS - 1):
        for r in range(2):
            c_copy(item, r).wait_send()
    for d in range(1, SIDE):
        gap1_copy(d).wait_send()
        gap2_copy(d).wait_send()
        gap2_arrived(d).wait_recv()
    for pair in range(PAIRS):
        gap = jnp.concatenate(
            [gap2[(pair * 2 + r) % SIDE, (pair * 2 + r) // SIDE] for r in range(2)], axis=0
        )
        gap = jnp.concatenate([gap, gap], axis=1)
        for h in range(2):
            span = slice(h * HALF, (h + 1) * HALF)
            out_ref[pair * 16 : (pair + 1) * 16, span] = (
                fin[h * PAIRS + pair] / (gap + colgap_ref[:, span])
            ).astype(jnp.bfloat16)


def on_device(amp_tiles, tile_pos, tile_count, cycle_integrals, row_gap, col_gap):
    f32, i16, bf16 = jnp.float32, jnp.int16, jnp.bfloat16
    vmem = pl.BlockSpec(memory_space=pltpu.VMEM)
    hbm = pl.BlockSpec(memory_space=pl.ANY)
    dma = pltpu.SemaphoreType.DMA
    block = (16, HALF)
    return pl.pallas_call(
        kernel,
        out_shape=jax.ShapeDtypeStruct((OWNERS * 8, COLS), bf16),
        in_specs=[hbm, hbm, vmem, vmem, hbm, hbm],
        out_specs=vmem,
        scratch_shapes=[
            pltpu.SMEM((OWNERS, CAP), jnp.int32),
            pltpu.SMEM((1, OWNERS), jnp.int32),
            pltpu.SMEM((OWNERS * CAP,), jnp.int32),
            pltpu.SMEM((OWNERS * CAP,), jnp.int32),
            pltpu.SMEM((OWNERS * ROWT_DEV,), jnp.int32),
            pltpu.VMEM((KT_DEV, TILE, HALF), bf16),
            pltpu.VMEM((KT_DEV, TILE, HALF), bf16),
            pltpu.VMEM((2, 2, CAP, TILE, TILE), bf16),
            pltpu.VMEM((CAP + 1, TILE, HALF), f32),
            pltpu.VMEM((OWN, 64, *block), f32),
            pltpu.VMEM((2, 2, 64, 8, HALF), f32),
            pltpu.VMEM((2, 2, 64, 8, HALF), f32),
            pltpu.VMEM((KEEP, 16, *block), f32),
            pltpu.VMEM((SLOTS, 2, 9, *block), i16),
            pltpu.VMEM((ITEMS, 2, 9, *block), i16),
            pltpu.VMEM((SLOTS, 2, 17, *block), i16),
            pltpu.VMEM((LAND, 2, 17, *block), i16),
            pltpu.VMEM((SLOTS, 2, 3, *block), i16),
            pltpu.VMEM((ITEMS, 2, 3, *block), i16),
            pltpu.VMEM((SLOTS, 2, 5, *block), i16),
            pltpu.VMEM((ITEMS, 2, 5, *block), i16),
            pltpu.VMEM((CBUF, SIDE, *block), f32),
            pltpu.VMEM((ITEMS, 3, *block), f32),
            pltpu.VMEM((ITEMS, *block), f32),
            pltpu.VMEM((OWNERS, 8, TILE), f32),
            pltpu.VMEM((SIDE, SIDE, 8, TILE), f32),
            pltpu.VMEM((SIDE, SIDE, 8, TILE), f32),
            dma((2,)),
            dma((2, W_PARTS)),
            dma((2,)),
            dma((2, 2)),
            dma((2, 2)),
            dma((SLOTS, 2)),
            dma((ITEMS, 2)),
            dma((SLOTS, 2)),
            dma((LAND, 2)),
            dma((SLOTS, 2)),
            dma((ITEMS, 2)),
            dma((SLOTS, 2)),
            dma((ITEMS, 2)),
            dma((CBUF, 3)),
            dma((ITEMS, 3)),
            dma((3,)),
            dma((3,)),
            dma((3,)),
            dma((3,)),
            pltpu.SemaphoreType.REGULAR,
        ],
        compiler_params=pltpu.CompilerParams(
            collective_id=0, has_side_effects=True, vmem_limit_bytes=63 * 1024 * 1024
        ),
        name="cycle_reduce",
    )(
        tile_pos,
        tile_count,
        row_gap.reshape(1, TILE),
        col_gap.reshape(1, COLS),
        amp_tiles.reshape(OWNERS, CAP, TILE, TILE),
        cycle_integrals.reshape(KT_DEV, TILE, COLS),
    )


def solution(mesh):
    return jax.shard_map(
        on_device,
        mesh=mesh,
        in_specs=(
            P("row", "ck", None, None, None, None),
            P(None, "ck", None, None),
            P(None, "ck", None),
            P("ck", None),
            P(("row", "ck")),
            P(),
        ),
        out_specs=P(("row", "ck"), None),
        check_vma=False,
    )
```

```python
import math

import jax
import jax.numpy as jnp
from jax import lax
from jax.experimental import pallas as pl
from jax.experimental.pallas import tpu as pltpu
from jax.sharding import PartitionSpec as P

TILE = 128
KT_DEV = 288
ROWT_DEV = 8
CAP = 16
COLS = 512
OWNERS = 16
HALF = COLS // 2
MESH = pl.DeviceIdType.MESH

SIDE = 4
PAIRS = OWNERS // 2
ITEMS = 2 * PAIRS
LAG_1, LAG_2, LAG_3 = 5, 4, 4
KEEP = LAG_1 + LAG_2
SLOTS = 4
W_PARTS = 4

LEVELS = 32000.0
STEPS = 256.0
LN2 = math.log(2.0)
FLOOR = 2.0**-100


def pick(a):
    return lax.div(2 - a, 2), lax.rem(a, 2), lax.div(a, 2)


def scale_code(top):
    level = jnp.ceil(jnp.log(jnp.maximum(top, FLOOR)) * (STEPS / LN2))
    return level.astype(jnp.int32).astype(jnp.int16), jnp.exp(level * (-LN2 / STEPS)) * LEVELS


def scale_value(code):
    level = code.astype(jnp.int32).astype(jnp.float32)
    return jnp.exp(level * (LN2 / STEPS)) * (1.0 / LEVELS)


def encode(block, inverse):
    return jnp.round(block * inverse).astype(jnp.int32).astype(jnp.int16)


def decode(block, scale):
    return block.astype(jnp.int32).astype(jnp.float32) * scale


def send_code(blocks, top, count, target):
    code, inverse = scale_code(top)
    for b in range(count):
        target[b] = encode(blocks(b), inverse)
    target[count] = code


def kernel(
    pos_ref, count_ref, rowgap_ref, colgap_ref, amp_ref, w_ref, out_ref,
    pos_s, count_s, ck_s, prev_s, last_s,
    w0_v, w1_v, amp_v, acc, own, csend, crecv, keep, s1send, s1recv, s2send, s2recv, cbuf, s3recv, fin, gap0, gap1, gap2,
    t_sem, w_sem, amp_sem, c_ssem, c_rsem, s1_ssem, s1_rsem, s2_ssem, s2_rsem,
    s3_ssem, s3_rsem, g1_ssem, g1_rsem, g2_ssem, g2_rsem, credit,
):
    row, ck = lax.axis_index("row"), lax.axis_index("ck")
    x, y = lax.div(row, SIDE), lax.rem(row, SIDE)
    z, core = lax.div(ck, 2), lax.rem(ck, 2)
    partner = (row, z * 2 + (1 - core))

    def w_copy(h, part):
        span = pl.ds(part * (KT_DEV // W_PARTS), KT_DEV // W_PARTS)
        return pltpu.make_async_copy(
            w_ref.at[span, :, h * HALF : (h + 1) * HALF], (w0_v, w1_v)[h].at[span], w_sem.at[h, part]
        )

    def amp_copy(item):
        slot = lax.rem(item, 2)
        return pltpu.make_async_copy(amp_ref.at[pl.ds(lax.rem(item, PAIRS) * 2, 2)], amp_v.at[slot], amp_sem.at[slot])

    pos_copy = pltpu.make_async_copy(pos_ref.at[row, 0], pos_s, t_sem.at[0])
    count_copy = pltpu.make_async_copy(count_ref.at[row], count_s, t_sem.at[1])
    pos_copy.start()
    count_copy.start()
    for h in range(2):
        for part in range(W_PARTS):
            w_copy(h, part).start()
        if h == 0:
            amp_copy(0).start()

    def on_axis(a):
        e0, e1, e2 = pick(a)
        return e0 * z + e1 * x + e2 * y

    def axis_peer(a, d):
        e0, e1, e2 = pick(a)
        mine = e0 * z + e1 * x + e2 * y
        shift = lax.rem(mine + d, SIDE) - mine
        return ((x + e1 * shift) * SIDE + y + e2 * shift, (z + e0 * shift) * 2 + core)

    def axis_of(item, stage):
        return lax.rem(lax.rem(item, 3) + stage, 3)

    barrier = pltpu.get_barrier_semaphore()
    pl.semaphore_signal(barrier, inc=1, device_id=partner, device_id_type=MESH)
    for a in range(3):
        for d in range(1, SIDE):
            pl.semaphore_signal(barrier, inc=1, device_id=axis_peer(a, d), device_id_type=MESH)

    lanes = lax.broadcasted_iota(jnp.int32, (8, TILE), 1)
    rows = lax.broadcasted_iota(jnp.int32, (8, TILE), 0)
    gap_row = jnp.broadcast_to(rowgap_ref[...], (8, TILE))
    for r in range(OWNERS):
        value = jnp.sum(jnp.where(lanes == rows + r * 8, gap_row, 0.0), axis=1, keepdims=True)
        gap0[r] = jnp.broadcast_to(value, (8, TILE))
    for b in range(SIDE):
        gap1[x, b] = gap0[x * SIDE + b]
    acc[CAP] = jnp.zeros((TILE, HALF), jnp.float32)
    pl.semaphore_wait(barrier, 10)

    def gap1_copy(d):
        return pltpu.make_async_remote_copy(
            src_ref=gap0.at[pl.ds(lax.rem(x + d, SIDE) * SIDE, SIDE)], dst_ref=gap1.at[x],
            send_sem=g1_ssem.at[d - 1], recv_sem=g1_rsem.at[d - 1], device_id=axis_peer(1, d), device_id_type=MESH,
        )

    def gap1_arrived(d):
        return pltpu.make_async_remote_copy(
            src_ref=gap0.at[pl.ds(0, SIDE)], dst_ref=gap1.at[lax.rem(x + SIDE - d, SIDE)],
            send_sem=g1_ssem.at[d - 1], recv_sem=g1_rsem.at[d - 1], device_id=axis_peer(1, d), device_id_type=MESH,
        )

    def gap2_copy(d):
        return pltpu.make_async_remote_copy(
            src_ref=gap1.at[:, lax.rem(y + d, SIDE)], dst_ref=gap2.at[y],
            send_sem=g2_ssem.at[d - 1], recv_sem=g2_rsem.at[d - 1], device_id=axis_peer(2, d), device_id_type=MESH,
        )

    def gap2_arrived(d):
        return pltpu.make_async_remote_copy(
            src_ref=gap1.at[:, 0], dst_ref=gap2.at[lax.rem(y + SIDE - d, SIDE)],
            send_sem=g2_ssem.at[d - 1], recv_sem=g2_rsem.at[d - 1], device_id=axis_peer(2, d), device_id_type=MESH,
        )

    for d in range(1, SIDE):
        gap1_copy(d).start()

    pos_copy.wait()
    count_copy.wait()

    def tables(owner, carry):
        live = count_s[0, owner]
        tiles = []
        for j in range(CAP):
            position = pos_s[owner, j]
            row_tile = lax.div(position, KT_DEV)
            ck_s[owner * CAP + j] = position - row_tile * KT_DEV
            row_tile = jnp.where(j < live, row_tile, -1 - j)
            before = jnp.int32(CAP)
            for k in range(j):
                before = jnp.where(tiles[k] == row_tile, k, before)
            prev_s[owner * CAP + j] = before
            tiles.append(row_tile)
        for i in range(ROWT_DEV):
            last = jnp.int32(CAP)
            for k in range(CAP):
                last = jnp.where(tiles[k] == i, k, last)
            last_s[owner * ROWT_DEV + i] = last
        return carry

    lax.fori_loop(0, OWNERS, tables, 0)

    for d in range(1, SIDE):
        gap1_arrived(d).wait_recv()
    for b in range(SIDE):
        gap2[y, b] = gap1[b, y]
    for d in range(1, SIDE):
        gap2_copy(d).start()

    def c_copy(item, r):
        slot = lax.rem(item, 2)
        return pltpu.make_async_remote_copy(
            src_ref=csend.at[slot, r], dst_ref=crecv.at[slot, r], send_sem=c_ssem.at[slot, r],
            recv_sem=c_rsem.at[slot, r], device_id=partner, device_id_type=MESH,
        )

    def coded_copy(item, d, stage, source, target, ssem, rsem):
        slot = lax.rem(item, SLOTS)
        return pltpu.make_async_remote_copy(
            src_ref=source.at[slot, d - 1], dst_ref=target.at[item, d - 1], send_sem=ssem.at[slot, d - 1],
            recv_sem=rsem.at[item, d - 1], device_id=axis_peer(axis_of(item, stage), d), device_id_type=MESH,
        )

    def s1_copy(item, d):
        return coded_copy(item, d, 0, s1send, s1recv, s1_ssem, s1_rsem)

    def s2_copy(item, d):
        return coded_copy(item, d, 1, s2send, s2recv, s2_ssem, s2_rsem)

    def s3_copy(item, d):
        slot = lax.rem(item, SLOTS)
        a = axis_of(item, 2)
        return pltpu.make_async_remote_copy(
            src_ref=cbuf.at[slot, lax.rem(on_axis(a) + d, SIDE)], dst_ref=s3recv.at[item, d - 1],
            send_sem=s3_ssem.at[slot, d - 1], recv_sem=s3_rsem.at[item, d - 1],
            device_id=axis_peer(a, d), device_id_type=MESH,
        )

    others = range(1, SIDE)

    def sent_before(item, copy, slots, which):
        @pl.when(item >= slots)
        def _():
            for d in which:
                copy(item - slots, d).wait_send()

    def compute(item):
        slot, oslot = lax.rem(item, 2), lax.rem(item, 2)
        h, pair = lax.div(item, PAIRS), lax.rem(item, PAIRS)

        @pl.when(item + 1 < ITEMS)
        def _():
            amp_copy(item + 1).start()

        for half in range(2):

            @pl.when(item == half * PAIRS)
            def _():
                for part in range(W_PARTS):
                    w_copy(half, part).wait()

        amp_copy(item).wait()
        sent_before(item, c_copy, 2, range(2))

        @pl.when(item >= 2)
        def _():
            pl.semaphore_wait(credit, 1)

        kind = lax.rem(item, 3)
        strides = []
        for a in range(3):
            e0, e1, e2 = pick(lax.rem(a - kind + 3, 3))
            strides.append(e0 * 16 + e1 * 4 + e2)
        sz, sx, sy = strides
        for r in range(2):
            owner = pair * 2 + r
            for half, w_v in enumerate((w0_v, w1_v)):

                @pl.when(h == half)
                def _():
                    for j in range(CAP):
                        at = owner * CAP + j
                        product = jnp.dot(amp_v[slot, r, j], w_v[ck_s[at]], preferred_element_type=jnp.float32)
                        acc[j] = product + acc[prev_s[at]]

            def spread(tz, carry):
                for side in range(2):
                    source = last_s[owner * ROWT_DEV + tz * 2 + (core if side == 0 else 1 - core)]
                    for tx in range(SIDE):
                        for ty in range(SIDE):
                            at = tx * SIDE + ty
                            place = tz * sz + tx * sx + ty * sy
                            if side == 0:
                                own[oslot, place, r * 8 : (r + 1) * 8] = acc[source, at * 8 : (at + 1) * 8]
                            else:
                                csend[slot, r, place] = acc[source, at * 8 : (at + 1) * 8]
                return carry

            lax.fori_loop(0, SIDE, spread, 0)
            c_copy(item, r).start()

    def stage1(item):
        slot, kslot, sslot = lax.rem(item, 2), lax.rem(item, KEEP), lax.rem(item, SLOTS)
        mine = on_axis(axis_of(item, 0))
        for r in range(2):
            c_copy(item, r).wait_recv()
        sent_before(item, s1_copy, SLOTS, others)

        def both(at):
            return own[slot, at] + jnp.concatenate([crecv[slot, 0, at], crecv[slot, 1, at]], axis=0)

        for d in (2, 1, 3):
            base = lax.rem(mine + d, SIDE) * 16
            top = jnp.zeros((16, HALF), jnp.float32)
            for b in range(16):
                total = both(base + b)
                own[slot, base + b] = total
                top = jnp.maximum(top, jnp.abs(total))
            send_code(lambda b, base=base: own[slot, base + b], top, 16, s1send.at[sslot, d - 1])
            s1_copy(item, d).start()
        for b in range(16):
            keep[kslot, b] = both(mine * 16 + b)

        @pl.when(item < ITEMS - 2)
        def _():
            pl.semaphore_signal(credit, inc=1, device_id=partner, device_id_type=MESH)

    def stage2(item):
        kslot, sslot = lax.rem(item, KEEP), lax.rem(item, SLOTS)
        mine = on_axis(axis_of(item, 1))
        for d in others:
            s1_copy(item, d).wait_recv()
        sent_before(item, s2_copy, SLOTS, others)
        scales = [scale_value(s1recv[item, d, 16]) for d in range(3)]

        def all_of(at):
            total = keep[kslot, at]
            for d in range(3):
                total = total + decode(s1recv[item, d, at], scales[d])
            return total

        for d in (2, 1, 3):
            base = lax.rem(mine + d, SIDE) * SIDE
            top = jnp.zeros((16, HALF), jnp.float32)
            for b in range(SIDE):
                total = all_of(base + b)
                keep[kslot, base + b] = total
                top = jnp.maximum(top, jnp.abs(total))
            send_code(lambda b, base=base: keep[kslot, base + b], top, SIDE, s2send.at[sslot, d - 1])
            s2_copy(item, d).start()
        for b in range(SIDE):
            keep[kslot, mine * SIDE + b] = all_of(mine * SIDE + b)

    def stage3(item):
        kslot, sslot = lax.rem(item, KEEP), lax.rem(item, SLOTS)
        mine = on_axis(axis_of(item, 1))
        for d in others:
            s2_copy(item, d).wait_recv()
        sent_before(item, s3_copy, SLOTS, others)
        scales = [scale_value(s2recv[item, d, SIDE]) for d in range(3)]
        for b in range(SIDE):
            total = keep[kslot, mine * SIDE + b]
            for d in range(3):
                total = total + decode(s2recv[item, d, b], scales[d])
            cbuf[sslot, b] = total
        for d in others:
            s3_copy(item, d).start()

    def finish(item):
        for d in range(1, SIDE):
            s3_copy(item, d).wait_recv()
        total = cbuf[lax.rem(item, SLOTS), on_axis(axis_of(item, 2))]
        for d in range(3):
            total = total + s3recv[item, d]
        fin[item] = total

    order = [
        (1 + LAG_1 + LAG_2 + LAG_3, finish), (1 + LAG_1 + LAG_2, stage3), (1 + LAG_1, stage2), (0, compute), (1, stage1),
    ]

    def step(t, carry):
        for first, body in order:
            pl.when((t >= first) & (t < first + ITEMS))(lambda first=first, body=body: body(t - first))
        return carry

    lax.fori_loop(0, ITEMS + 1 + LAG_1 + LAG_2 + LAG_3, step, 0)

    def drain(item, carry):
        for copy in (s1_copy, s2_copy, s3_copy):
            for d in others:
                copy(item, d).wait_send()
        return carry

    lax.fori_loop(ITEMS - SLOTS, ITEMS, drain, 0)
    for item in (ITEMS - 2, ITEMS - 1):
        for r in range(2):
            c_copy(item, r).wait_send()
    for d in range(1, SIDE):
        gap1_copy(d).wait_send()
        gap2_copy(d).wait_send()
        gap2_arrived(d).wait_recv()
    for pair in range(PAIRS):
        gap = jnp.concatenate(
            [gap2[(pair * 2 + r) % SIDE, (pair * 2 + r) // SIDE] for r in range(2)], axis=0
        )
        gap = jnp.concatenate([gap, gap], axis=1)
        for h in range(2):
            span = slice(h * HALF, (h + 1) * HALF)
            out_ref[pair * 16 : (pair + 1) * 16, span] = (
                fin[h * PAIRS + pair] / (gap + colgap_ref[:, span])
            ).astype(jnp.bfloat16)


def on_device(amp_tiles, tile_pos, tile_count, cycle_integrals, row_gap, col_gap):
    f32, i16, bf16 = jnp.float32, jnp.int16, jnp.bfloat16
    vmem = pl.BlockSpec(memory_space=pltpu.VMEM)
    hbm = pl.BlockSpec(memory_space=pl.ANY)
    dma = pltpu.SemaphoreType.DMA
    block = (16, HALF)
    return pl.pallas_call(
        kernel,
        out_shape=jax.ShapeDtypeStruct((OWNERS * 8, COLS), bf16),
        in_specs=[hbm, hbm, vmem, vmem, hbm, hbm],
        out_specs=vmem,
        scratch_shapes=[
            pltpu.SMEM((OWNERS, CAP), jnp.int32),
            pltpu.SMEM((1, OWNERS), jnp.int32),
            pltpu.SMEM((OWNERS * CAP,), jnp.int32),
            pltpu.SMEM((OWNERS * CAP,), jnp.int32),
            pltpu.SMEM((OWNERS * ROWT_DEV,), jnp.int32),
            pltpu.VMEM((KT_DEV, TILE, HALF), bf16),
            pltpu.VMEM((KT_DEV, TILE, HALF), bf16),
            pltpu.VMEM((2, 2, CAP, TILE, TILE), bf16),
            pltpu.VMEM((CAP + 1, TILE, HALF), f32),
            pltpu.VMEM((2, 64, *block), f32),
            pltpu.VMEM((2, 2, 64, 8, HALF), f32),
            pltpu.VMEM((2, 2, 64, 8, HALF), f32),
            pltpu.VMEM((KEEP, 16, *block), f32),
            pltpu.VMEM((SLOTS, 3, 17, *block), i16),
            pltpu.VMEM((ITEMS, 3, 17, *block), i16),
            pltpu.VMEM((SLOTS, 3, 5, *block), i16),
            pltpu.VMEM((ITEMS, 3, 5, *block), i16),
            pltpu.VMEM((SLOTS, SIDE, *block), f32),
            pltpu.VMEM((ITEMS, 3, *block), f32),
            pltpu.VMEM((ITEMS, *block), f32),
            pltpu.VMEM((OWNERS, 8, TILE), f32),
            pltpu.VMEM((SIDE, SIDE, 8, TILE), f32),
            pltpu.VMEM((SIDE, SIDE, 8, TILE), f32),
            dma((2,)),
            dma((2, W_PARTS)),
            dma((2,)),
            dma((2, 2)),
            dma((2, 2)),
            dma((SLOTS, 3)),
            dma((ITEMS, 3)),
            dma((SLOTS, 3)),
            dma((ITEMS, 3)),
            dma((SLOTS, 3)),
            dma((ITEMS, 3)),
            dma((3,)),
            dma((3,)),
            dma((3,)),
            dma((3,)),
            pltpu.SemaphoreType.REGULAR,
        ],
        compiler_params=pltpu.CompilerParams(
            collective_id=0, has_side_effects=True, vmem_limit_bytes=63 * 1024 * 1024
        ),
        name="cycle_reduce",
    )(
        tile_pos,
        tile_count,
        row_gap.reshape(1, TILE),
        col_gap.reshape(1, COLS),
        amp_tiles.reshape(OWNERS, CAP, TILE, TILE),
        cycle_integrals.reshape(KT_DEV, TILE, COLS),
    )


def solution(mesh):
    return jax.shard_map(
        on_device,
        mesh=mesh,
        in_specs=(
            P("row", "ck", None, None, None, None),
            P(None, "ck", None, None),
            P(None, "ck", None),
            P("ck", None),
            P(("row", "ck")),
            P(),
        ),
        out_specs=P(("row", "ck"), None),
        check_vma=False,
    )
```

```python
import math

import jax
import jax.numpy as jnp
from jax import lax
from jax.experimental import pallas as pl
from jax.experimental.pallas import tpu as pltpu
from jax.sharding import PartitionSpec as P

TILE = 128
KT_DEV = 288
ROWT_DEV = 8
CAP = 16
COLS = 512
OWNERS = 16
HALF = COLS // 2
MESH = pl.DeviceIdType.MESH

SIDE = 4
PAIRS = OWNERS // 2
ITEMS = 2 * PAIRS
LAG_C, LAG_1A, LAG_1B, LAG_2A, LAG_2B, LAG_3 = 1, 4, 4, 4, 5, 5
OWN = LAG_1A + LAG_C
KEEP = LAG_1B + LAG_2A
CBUF = LAG_2B + LAG_3
SLOTS = 4
LAND = LAG_1A + LAG_1B
W_PARTS = 4
AROUND = (1, 3)

LEVELS = 32000.0
STEPS = 256.0
LN2 = math.log(2.0)
FLOOR = 2.0**-100


def pick(a):
    return lax.div(2 - a, 2), lax.rem(a, 2), lax.div(a, 2)


def scale_code(top):
    level = jnp.ceil(jnp.log(jnp.maximum(top, FLOOR)) * (STEPS / LN2))
    return level.astype(jnp.int32).astype(jnp.int16), jnp.exp(level * (-LN2 / STEPS)) * LEVELS


def scale_value(code):
    level = code.astype(jnp.int32).astype(jnp.float32)
    return jnp.exp(level * (LN2 / STEPS)) * (1.0 / LEVELS)


def encode(block, inverse):
    return jnp.round(block * inverse).astype(jnp.int32).astype(jnp.int16)


def decode(block, scale):
    return block.astype(jnp.int32).astype(jnp.float32) * scale


def send_code(read, count, target):
    top = jnp.abs(read(0))
    for b in range(1, count):
        top = jnp.maximum(top, jnp.abs(read(b)))
    code, inverse = scale_code(top)
    for b in range(count):
        target[b] = encode(read(b), inverse)
    target[count] = code


def kernel(
    pos_ref, count_ref, rowgap_ref, colgap_ref, amp_ref, w_ref, out_ref,
    pos_s, count_s, ck_s, prev_s, last_s,
    w0_v, w1_v, amp_v, acc, own, csend, crecv, keep, a1send, a1recv, b1send, b1recv,
    a2send, a2recv, b2send, b2recv, cbuf, s3recv, fin, gap0, gap1, gap2,
    t_sem, w_sem, amp_sem, c_ssem, c_rsem, a1_ssem, a1_rsem, b1_ssem, b1_rsem,
    a2_ssem, a2_rsem, b2_ssem, b2_rsem, s3_ssem, s3_rsem, g1_ssem, g1_rsem, g2_ssem, g2_rsem, credit,
):
    row, ck = lax.axis_index("row"), lax.axis_index("ck")
    x, y = lax.div(row, SIDE), lax.rem(row, SIDE)
    z, core = lax.div(ck, 2), lax.rem(ck, 2)
    partner = (row, z * 2 + (1 - core))

    def w_copy(h, part):
        span = pl.ds(part * (KT_DEV // W_PARTS), KT_DEV // W_PARTS)
        return pltpu.make_async_copy(
            w_ref.at[span, :, h * HALF : (h + 1) * HALF], (w0_v, w1_v)[h].at[span], w_sem.at[h, part]
        )

    def amp_copy(item):
        slot = lax.rem(item, 2)
        return pltpu.make_async_copy(amp_ref.at[pl.ds(lax.rem(item, PAIRS) * 2, 2)], amp_v.at[slot], amp_sem.at[slot])

    pos_copy = pltpu.make_async_copy(pos_ref.at[row, 0], pos_s, t_sem.at[0])
    count_copy = pltpu.make_async_copy(count_ref.at[row], count_s, t_sem.at[1])
    pos_copy.start()
    count_copy.start()
    amp_copy(0).start()
    for part in range(W_PARTS):
        w_copy(0, part).start()

    def on_axis(a):
        e0, e1, e2 = pick(a)
        return e0 * z + e1 * x + e2 * y

    def axis_peer(a, d):
        e0, e1, e2 = pick(a)
        mine = e0 * z + e1 * x + e2 * y
        shift = lax.rem(mine + d, SIDE) - mine
        return ((x + e1 * shift) * SIDE + y + e2 * shift, (z + e0 * shift) * 2 + core)

    def axis_of(item, stage):
        return lax.rem(lax.rem(item, 3) + stage, 3)

    barrier = pltpu.get_barrier_semaphore()
    pl.semaphore_signal(barrier, inc=1, device_id=partner, device_id_type=MESH)
    for a in range(3):
        for d in range(1, SIDE):
            pl.semaphore_signal(barrier, inc=1, device_id=axis_peer(a, d), device_id_type=MESH)

    lanes = lax.broadcasted_iota(jnp.int32, (8, TILE), 1)
    rows = lax.broadcasted_iota(jnp.int32, (8, TILE), 0)
    gap_row = jnp.broadcast_to(rowgap_ref[...], (8, TILE))
    for r in range(OWNERS):
        value = jnp.sum(jnp.where(lanes == rows + r * 8, gap_row, 0.0), axis=1, keepdims=True)
        gap0[r] = jnp.broadcast_to(value, (8, TILE))
    for b in range(SIDE):
        gap1[x, b] = gap0[x * SIDE + b]
    acc[CAP] = jnp.zeros((TILE, HALF), jnp.float32)
    pl.semaphore_wait(barrier, 10)

    def gap1_copy(d):
        return pltpu.make_async_remote_copy(
            src_ref=gap0.at[pl.ds(lax.rem(x + d, SIDE) * SIDE, SIDE)], dst_ref=gap1.at[x],
            send_sem=g1_ssem.at[d - 1], recv_sem=g1_rsem.at[d - 1], device_id=axis_peer(1, d), device_id_type=MESH,
        )

    def gap1_arrived(d):
        return pltpu.make_async_remote_copy(
            src_ref=gap0.at[pl.ds(0, SIDE)], dst_ref=gap1.at[lax.rem(x + SIDE - d, SIDE)],
            send_sem=g1_ssem.at[d - 1], recv_sem=g1_rsem.at[d - 1], device_id=axis_peer(1, d), device_id_type=MESH,
        )

    def gap2_copy(d):
        return pltpu.make_async_remote_copy(
            src_ref=gap1.at[:, lax.rem(y + d, SIDE)], dst_ref=gap2.at[y],
            send_sem=g2_ssem.at[d - 1], recv_sem=g2_rsem.at[d - 1], device_id=axis_peer(2, d), device_id_type=MESH,
        )

    def gap2_arrived(d):
        return pltpu.make_async_remote_copy(
            src_ref=gap1.at[:, 0], dst_ref=gap2.at[lax.rem(y + SIDE - d, SIDE)],
            send_sem=g2_ssem.at[d - 1], recv_sem=g2_rsem.at[d - 1], device_id=axis_peer(2, d), device_id_type=MESH,
        )

    for d in range(1, SIDE):
        gap1_copy(d).start()

    pos_copy.wait()
    count_copy.wait()

    def tables(owner, carry):
        live = count_s[0, owner]
        tiles = []
        for j in range(CAP):
            position = pos_s[owner, j]
            row_tile = lax.div(position, KT_DEV)
            ck_s[owner * CAP + j] = position - row_tile * KT_DEV
            row_tile = jnp.where(j < live, row_tile, -1 - j)
            before = jnp.int32(CAP)
            for k in range(j):
                before = jnp.where(tiles[k] == row_tile, k, before)
            prev_s[owner * CAP + j] = before
            tiles.append(row_tile)
        for i in range(ROWT_DEV):
            last = jnp.int32(CAP)
            for k in range(CAP):
                last = jnp.where(tiles[k] == i, k, last)
            last_s[owner * ROWT_DEV + i] = last
        return carry

    lax.fori_loop(0, OWNERS, tables, 0)

    for d in range(1, SIDE):
        gap1_arrived(d).wait_recv()
    for b in range(SIDE):
        gap2[y, b] = gap1[b, y]
    for d in range(1, SIDE):
        gap2_copy(d).start()

    def c_copy(item, r):
        slot = lax.rem(item, 2)
        return pltpu.make_async_remote_copy(
            src_ref=csend.at[slot, r], dst_ref=crecv.at[slot, r], send_sem=c_ssem.at[slot, r],
            recv_sem=c_rsem.at[slot, r], device_id=partner, device_id_type=MESH,
        )

    def ring_copy(item, way, stage, source, target, ssem, rsem, slots=ITEMS):
        slot, land = lax.rem(item, SLOTS), lax.rem(item, slots)
        return pltpu.make_async_remote_copy(
            src_ref=source.at[slot, way], dst_ref=target.at[land, way], send_sem=ssem.at[slot, way],
            recv_sem=rsem.at[land, way], device_id=axis_peer(axis_of(item, stage), AROUND[way]), device_id_type=MESH,
        )

    def a1_copy(item, way):
        return ring_copy(item, way, 0, a1send, a1recv, a1_ssem, a1_rsem)

    def b1_copy(item, way):
        return ring_copy(item, way, 0, b1send, b1recv, b1_ssem, b1_rsem, LAND)

    def a2_copy(item, way):
        return ring_copy(item, way, 1, a2send, a2recv, a2_ssem, a2_rsem)

    def b2_copy(item, way):
        return ring_copy(item, way, 1, b2send, b2recv, b2_ssem, b2_rsem)

    def s3_copy(item, d):
        slot = lax.rem(item, CBUF)
        a = axis_of(item, 2)
        return pltpu.make_async_remote_copy(
            src_ref=cbuf.at[slot, lax.rem(on_axis(a) + d, SIDE)], dst_ref=s3recv.at[item, d - 1],
            send_sem=s3_ssem.at[slot, d - 1], recv_sem=s3_rsem.at[item, d - 1],
            device_id=axis_peer(a, d), device_id_type=MESH,
        )

    def sent_before(item, copy, slots):
        @pl.when(item >= slots)
        def _():
            for way in range(2):
                copy(item - slots, way).wait_send()

    def compute(item):
        slot, oslot = lax.rem(item, 2), lax.rem(item, OWN)
        h, pair = lax.div(item, PAIRS), lax.rem(item, PAIRS)

        @pl.when(item + 1 < ITEMS)
        def _():
            amp_copy(item + 1).start()

        for half in range(2):

            @pl.when(item == half * PAIRS)
            def _():
                for part in range(W_PARTS):
                    w_copy(half, part).wait()
                if half == 0:
                    for part in range(W_PARTS):
                        w_copy(1, part).start()

        amp_copy(item).wait()
        sent_before(item, c_copy, 2)

        @pl.when(item >= 2)
        def _():
            pl.semaphore_wait(credit, 1)

        kind = lax.rem(item, 3)
        strides = []
        for a in range(3):
            e0, e1, e2 = pick(lax.rem(a - kind + 3, 3))
            strides.append(e0 * 16 + e1 * 4 + e2)
        sz, sx, sy = strides
        for r in range(2):
            owner = pair * 2 + r
            for half, w_v in enumerate((w0_v, w1_v)):

                @pl.when(h == half)
                def _():
                    for j in range(CAP):
                        at = owner * CAP + j
                        product = jnp.dot(amp_v[slot, r, j], w_v[ck_s[at]], preferred_element_type=jnp.float32)
                        acc[j] = product + acc[prev_s[at]]

            def spread(tz, carry):
                for side in range(2):
                    source = last_s[owner * ROWT_DEV + tz * 2 + (core if side == 0 else 1 - core)]
                    for tx in range(SIDE):
                        for ty in range(SIDE):
                            at = tx * SIDE + ty
                            place = tz * sz + tx * sx + ty * sy
                            if side == 0:
                                own[oslot, place, r * 8 : (r + 1) * 8] = acc[source, at * 8 : (at + 1) * 8]
                            else:
                                csend[slot, r, place] = acc[source, at * 8 : (at + 1) * 8]
                return carry

            lax.fori_loop(0, SIDE, spread, 0)
            c_copy(item, r).start()

    def stage1a(item):
        slot, oslot, sslot = lax.rem(item, 2), lax.rem(item, OWN), lax.rem(item, SLOTS)
        mine = on_axis(axis_of(item, 0))
        for r in range(2):
            c_copy(item, r).wait_recv()
        sent_before(item, a1_copy, SLOTS)

        def both(at):
            for r in range(2):
                own[oslot, at, r * 8 : (r + 1) * 8] += crecv[slot, r, at]

        base = lax.rem(mine + 2, SIDE) * 16
        for way in range(2):
            start = base + way * 8
            for b in range(8):
                both(start + b)
            send_code(lambda b, start=start: own[oslot, start + b], 8, a1send.at[sslot, way])
            a1_copy(item, way).start()

        def rest(d, carry):
            at = lax.rem(mine + 3 + d, SIDE) * 16
            for b in range(16):
                both(at + b)
            return carry

        lax.fori_loop(0, 3, rest, 0)

        @pl.when(item < ITEMS - 2)
        def _():
            pl.semaphore_signal(credit, inc=1, device_id=partner, device_id_type=MESH)

    def pass_on(item, count, stage, source, arrived, sending, copy_a, copy_b):
        sslot = lax.rem(item, SLOTS)
        mine = on_axis(axis_of(item, stage))
        for way in range(2):
            copy_a(item, way).wait_recv()
        sent_before(item, copy_b, SLOTS)
        part = count // 2
        for way in range(2):
            base = lax.rem(mine + AROUND[way], SIDE) * count
            scale = scale_value(arrived[item, way, part])
            for b in range(part):
                source[base + way * part + b] += decode(arrived[item, way, b], scale)
            send_code(lambda b, base=base: source[base + b], count, sending.at[sslot, way])
            copy_b(item, way).start()
        return mine * count

    def stage1b(item):
        source = own.at[lax.rem(item, OWN)]
        base = pass_on(item, 16, 0, source, a1recv, b1send, a1_copy, b1_copy)
        kslot = lax.rem(item, KEEP)
        for b in range(16):
            keep[kslot, b] = source[base + b]

    def stage2a(item):
        source, sslot, land = keep.at[lax.rem(item, KEEP)], lax.rem(item, SLOTS), lax.rem(item, LAND)
        mine = on_axis(axis_of(item, 1))
        for way in range(2):
            b1_copy(item, way).wait_recv()
        sent_before(item, a2_copy, SLOTS)
        up, down = [scale_value(b1recv[land, way, 16]) for way in range(2)]

        def both(at):
            source[at] += decode(b1recv[land, 0, at], up) + decode(b1recv[land, 1, at], down)

        base = lax.rem(mine + 2, SIDE) * SIDE
        for b in range(SIDE):
            both(base + b)
        for way in range(2):
            start = base + way * 2
            send_code(lambda b, start=start: source[start + b], 2, a2send.at[sslot, way])
            a2_copy(item, way).start()
        for d in (3, 0, 1):
            base = lax.rem(mine + d, SIDE) * SIDE
            for b in range(SIDE):
                both(base + b)

    def stage2b(item):
        source, cslot = keep.at[lax.rem(item, KEEP)], lax.rem(item, CBUF)
        base = pass_on(item, SIDE, 1, source, a2recv, b2send, a2_copy, b2_copy)

        @pl.when(item >= CBUF)
        def _():
            for d in range(1, SIDE):
                s3_copy(item - CBUF, d).wait_send()

        for b in range(SIDE):
            cbuf[cslot, b] = source[base + b]

    def stage3(item):
        cslot = lax.rem(item, CBUF)
        for way in range(2):
            b2_copy(item, way).wait_recv()
        up, down = [scale_value(b2recv[item, way, SIDE]) for way in range(2)]
        for b in range(SIDE):
            cbuf[cslot, b] += decode(b2recv[item, 0, b], up) + decode(b2recv[item, 1, b], down)
        for d in range(1, SIDE):
            s3_copy(item, d).start()

    def finish(item):
        for d in range(1, SIDE):
            s3_copy(item, d).wait_recv()
        total = cbuf[lax.rem(item, CBUF), on_axis(axis_of(item, 2))]
        for d in range(3):
            total = total + s3recv[item, d]
        fin[item] = total

    stages = []
    lag = LAG_C
    for body, after in (
        (stage1a, LAG_1A), (stage1b, LAG_1B), (stage2a, LAG_2A), (stage2b, LAG_2B), (stage3, LAG_3), (finish, 0),
    ):
        stages.append((lag, body))
        lag += after
    order = [*reversed(stages[1:]), (0, compute), stages[0]]

    def step(t, carry):
        for first, body in order:
            pl.when((t >= first) & (t < first + ITEMS))(lambda first=first, body=body: body(t - first))
        return carry

    lax.fori_loop(0, ITEMS + lag, step, 0)

    def drain(item, carry):
        for way in range(2):
            for copy in (a1_copy, b1_copy, a2_copy, b2_copy):
                copy(item, way).wait_send()
        return carry

    lax.fori_loop(ITEMS - SLOTS, ITEMS, drain, 0)

    def drain3(item, carry):
        for d in range(1, SIDE):
            s3_copy(item, d).wait_send()
        return carry

    lax.fori_loop(ITEMS - CBUF, ITEMS, drain3, 0)
    for item in (ITEMS - 2, ITEMS - 1):
        for r in range(2):
            c_copy(item, r).wait_send()
    for d in range(1, SIDE):
        gap1_copy(d).wait_send()
        gap2_copy(d).wait_send()
        gap2_arrived(d).wait_recv()
    for pair in range(PAIRS):
        gap = jnp.concatenate(
            [gap2[(pair * 2 + r) % SIDE, (pair * 2 + r) // SIDE] for r in range(2)], axis=0
        )
        gap = jnp.concatenate([gap, gap], axis=1)
        for h in range(2):
            span = slice(h * HALF, (h + 1) * HALF)
            out_ref[pair * 16 : (pair + 1) * 16, span] = (
                fin[h * PAIRS + pair] / (gap + colgap_ref[:, span])
            ).astype(jnp.bfloat16)


def on_device(amp_tiles, tile_pos, tile_count, cycle_integrals, row_gap, col_gap):
    f32, i16, bf16 = jnp.float32, jnp.int16, jnp.bfloat16
    vmem = pl.BlockSpec(memory_space=pltpu.VMEM)
    hbm = pl.BlockSpec(memory_space=pl.ANY)
    dma = pltpu.SemaphoreType.DMA
    block = (16, HALF)
    return pl.pallas_call(
        kernel,
        out_shape=jax.ShapeDtypeStruct((OWNERS * 8, COLS), bf16),
        in_specs=[hbm, hbm, vmem, vmem, hbm, hbm],
        out_specs=vmem,
        scratch_shapes=[
            pltpu.SMEM((OWNERS, CAP), jnp.int32),
            pltpu.SMEM((1, OWNERS), jnp.int32),
            pltpu.SMEM((OWNERS * CAP,), jnp.int32),
            pltpu.SMEM((OWNERS * CAP,), jnp.int32),
            pltpu.SMEM((OWNERS * ROWT_DEV,), jnp.int32),
            pltpu.VMEM((KT_DEV, TILE, HALF), bf16),
            pltpu.VMEM((KT_DEV, TILE, HALF), bf16),
            pltpu.VMEM((2, 2, CAP, TILE, TILE), bf16),
            pltpu.VMEM((CAP + 1, TILE, HALF), f32),
            pltpu.VMEM((OWN, 64, *block), f32),
            pltpu.VMEM((2, 2, 64, 8, HALF), f32),
            pltpu.VMEM((2, 2, 64, 8, HALF), f32),
            pltpu.VMEM((KEEP, 16, *block), f32),
            pltpu.VMEM((SLOTS, 2, 9, *block), i16),
            pltpu.VMEM((ITEMS, 2, 9, *block), i16),
            pltpu.VMEM((SLOTS, 2, 17, *block), i16),
            pltpu.VMEM((LAND, 2, 17, *block), i16),
            pltpu.VMEM((SLOTS, 2, 3, *block), i16),
            pltpu.VMEM((ITEMS, 2, 3, *block), i16),
            pltpu.VMEM((SLOTS, 2, 5, *block), i16),
            pltpu.VMEM((ITEMS, 2, 5, *block), i16),
            pltpu.VMEM((CBUF, SIDE, *block), f32),
            pltpu.VMEM((ITEMS, 3, *block), f32),
            pltpu.VMEM((ITEMS, *block), f32),
            pltpu.VMEM((OWNERS, 8, TILE), f32),
            pltpu.VMEM((SIDE, SIDE, 8, TILE), f32),
            pltpu.VMEM((SIDE, SIDE, 8, TILE), f32),
            dma((2,)),
            dma((2, W_PARTS)),
            dma((2,)),
            dma((2, 2)),
            dma((2, 2)),
            dma((SLOTS, 2)),
            dma((ITEMS, 2)),
            dma((SLOTS, 2)),
            dma((LAND, 2)),
            dma((SLOTS, 2)),
            dma((ITEMS, 2)),
            dma((SLOTS, 2)),
            dma((ITEMS, 2)),
            dma((CBUF, 3)),
            dma((ITEMS, 3)),
            dma((3,)),
            dma((3,)),
            dma((3,)),
            dma((3,)),
            pltpu.SemaphoreType.REGULAR,
        ],
        compiler_params=pltpu.CompilerParams(
            collective_id=0, has_side_effects=True, vmem_limit_bytes=63 * 1024 * 1024
        ),
        name="cycle_reduce",
    )(
        tile_pos,
        tile_count,
        row_gap.reshape(1, TILE),
        col_gap.reshape(1, COLS),
        amp_tiles.reshape(OWNERS, CAP, TILE, TILE),
        cycle_integrals.reshape(KT_DEV, TILE, COLS),
    )


def solution(mesh):
    return jax.shard_map(
        on_device,
        mesh=mesh,
        in_specs=(
            P("row", "ck", None, None, None, None),
            P(None, "ck", None, None),
            P(None, "ck", None),
            P("ck", None),
            P(("row", "ck")),
            P(),
        ),
        out_specs=P(("row", "ck"), None),
        check_vma=False,
    )
```
